128 devices in a mesh: leaf: 128 (over x, y, z, core).
Axes of the slice: x: 4, y: 4, z: 4, core: 2. Of those that a mesh axis runs over, the one named last changes fastest.
Arguments:
- coords: float32 [6, 1048576], P(None, 'leaf'), may hold values from 0 to 4
- right_sides: float32 [8, 1048576], P(None, 'leaf'), may hold values from -6 to 6
- projection: float32 [1048576, 256], P('leaf'), may hold values from -0.0625 to 0.0625
- skel_index: int32 [128, 256], P('leaf'), may hold values from 0 to 8191
- selection: int32 [126, 256], replicated, may hold values from 0 to 511
- transfer: float32 [512, 256], replicated, may hold values from -0.25 to 0.25
- near_leaf: int32 [4096, 8], P('leaf'), may hold values from 0 to 4095, as said below
- near_count: int32 [4096], P('leaf'), may hold values from 1 to 8, as said below
Outputs:
- product: float32 [8, 1048576], P(None, 'leaf')
The draws below stay inside these ranges and needn't reach their ends.
Inputs may be any that keep to these rules, and one draw needn't show every extreme that they name: `near_leaf`: slot 0 of leaf g is g itself; every listed leaf is held by the device subtree of g or by one of the two subtrees next to it. `near_count`: all leaves of some device subtrees use all 8 slots; the others use up to 4.
All inputs are finite; a program needn't handle non-finite values.
Results may differ from the reference program's by a relative error of at most 0.0003.
Values sent between devices are 32-bit elements; how exact they have to be, the bound alone decides.
A program may use at most 192 MiB of HBM per device.

```python
import jax
import jax.numpy as jnp
from jax import lax

DIMS = 6
RHS = 8
LEAF = 256
RANK = 256
NEAR = 8
LEAVES_DEV = 32
PTS_DEV = 8192
LEAVES = 4096
POINTS = 1048576
LEVELS = 7
N_LEAF = 128


def draw_coords(key, part):
    key = jax.random.fold_in(key, 11)
    noise = jnp.clip(1.25 + 0.6 * jax.random.normal(key, (DIMS, POINTS), jnp.float32), 0.0, 2.5)
    device = jnp.arange(POINTS, dtype=jnp.int32) // PTS_DEV
    offsets = jnp.zeros((DIMS, POINTS), jnp.float32)
    rows = jnp.arange(DIMS, dtype=jnp.int32)
    for level in range(8):
        bit_on = (device // 2 ** level % 2).astype(jnp.float32)
        offsets = offsets + 0.6 * (rows[:, None] == level % DIMS).astype(jnp.float32) * bit_on[None, :]
    return noise + offsets


def draw_near_leaf(key, part):
    key = jax.random.fold_in(key, 23)
    key_side, key_local = jax.random.split(key)
    leaves = jnp.arange(LEAVES, dtype=jnp.int32)
    device = leaves // LEAVES_DEV
    side = jax.random.randint(key_side, (LEAVES, NEAR), -1, 2)
    owner = jnp.clip(device[:, None] + side, 0, N_LEAF - 1)
    local = jax.random.randint(key_local, (LEAVES, NEAR), 0, LEAVES_DEV)
    chosen = owner * LEAVES_DEV + local
    first = jnp.arange(NEAR, dtype=jnp.int32)[None, :] == 0
    return jnp.where(first, leaves[:, None], chosen).astype(jnp.int32)


def draw_near_count(key, part):
    key = jax.random.fold_in(key, 37)
    key_heavy, key_light = jax.random.split(key)
    device = jnp.arange(LEAVES, dtype=jnp.int32) // LEAVES_DEV
    heavy_dev = jax.random.randint(key_heavy, (N_LEAF,), 0, 4) == 0
    heavy_dev = heavy_dev | (jnp.arange(N_LEAF, dtype=jnp.int32) == 0)
    light = jax.random.randint(key_light, (LEAVES,), 1, NEAR // 2 + 1)
    return jnp.where(heavy_dev[device], NEAR, light).astype(jnp.int32)


def plant(result, stream_key, smallest, largest):
    place = [jax.random.randint(jax.random.fold_in(stream_key, axis), (), 0, length) for axis, length in enumerate(result.shape)]
    longest = result.shape.index(max(result.shape))
    next_to = place[:longest] + [(place[longest] + 1) % result.shape[longest]] + place[longest + 1:]
    return result.at[tuple(place)].set(smallest).at[tuple(next_to)].set(largest)


def shard_levels(rng, dims, shards, smallest, high):
    gain = 1.0
    for axis_at, shards_of in shards:
        draws = jax.random.uniform(jax.random.fold_in(jax.random.fold_in(rng, 6), axis_at), (shards_of,), jnp.float32, smallest / len(shards), high / len(shards))
        gain = gain * jnp.repeat(jnp.exp(draws), dims[axis_at] // shards_of).reshape((-1,) + (1,) * (len(dims) - 1 - axis_at))
    return gain


def bell_draw(own_key, shape, spread, most, shards=(), kind=jnp.bfloat16):
    values = jax.random.normal(own_key, shape, jnp.float32) * spread
    if len(shards) > 0:
        values = shard_levels(own_key, shape, shards, -0.22, 0.18) * values
    return jnp.clip(values, min=-most, max=most).astype(kind)


def setup_inputs(seed: int = 0) -> dict:
    seeds = jax.random.split(jax.random.key(seed), 9)
    coords = draw_coords(jax.random.fold_in(seeds[8], 71), 0)
    right_sides = bell_draw(seeds[1], (RHS, POINTS), 1.0, 6.0, ((1, 128),), jnp.float32)
    projection = bell_draw(seeds[2], (POINTS, RANK), PTS_DEV ** -0.5, 0.0625, ((0, 128),), jnp.float32)
    skel_index = plant(jax.random.randint(seeds[3], (N_LEAF, RANK), 0, PTS_DEV), jax.random.fold_in(seeds[3], 1), 0, PTS_DEV - 1).astype(jnp.int32)
    selection = plant(jax.random.randint(seeds[4], (N_LEAF - 2, RANK), 0, 2 * RANK), jax.random.fold_in(seeds[4], 1), 0, (2 * RANK) - 1).astype(jnp.int32)
    transfer = bell_draw(seeds[5], (2 * RANK, RANK), (2 * RANK) ** -0.5, 0.25, (), jnp.float32)
    near_leaf = draw_near_leaf(jax.random.fold_in(seeds[8], 71), 0)
    near_count = draw_near_count(jax.random.fold_in(seeds[8], 71), 0)
    return {"coords": coords, "right_sides": right_sides, "projection": projection, "skel_index": skel_index, "selection": selection, "transfer": transfer, "near_leaf": near_leaf, "near_count": near_count}


def kernel_block(sources, targets):
    dots = lax.dot_general(sources, targets, (((0,), (0,)), ((), ())), precision=lax.Precision.HIGHEST)
    src_sq = jnp.sum(sources * sources, axis=0)
    tgt_sq = jnp.sum(targets * targets, axis=0)
    distance = jnp.maximum(src_sq[:, None] + tgt_sq[None, :] - 2.0 * dots, 0.0)
    return jnp.exp(-0.5 * distance)


def reference(coords, right_sides, projection, skel_index, selection, transfer, near_leaf, near_count):
    leaf_coords = jnp.moveaxis(coords.reshape(DIMS, LEAVES, LEAF), 1, 0)
    leaf_values = jnp.moveaxis(right_sides.reshape(RHS, LEAVES, LEAF), 1, 0)

    def near_one(inputs):
        targets, sources_list, count = inputs

        def slot_term(source_leaf, slot):
            src_c = leaf_coords[source_leaf]
            src_x = leaf_values[source_leaf]
            block = kernel_block(src_c, targets)
            term = jnp.dot(src_x, block, precision=lax.Precision.HIGHEST)
            return jnp.where(slot < count, term, jnp.zeros_like(term))

        slots = jnp.arange(NEAR, dtype=jnp.int32)
        return jnp.sum(jax.vmap(slot_term)(sources_list, slots), axis=0)

    near = lax.map(near_one, (leaf_coords, near_leaf, near_count))
    near = jnp.moveaxis(near, 0, 1).reshape(RHS, POINTS)

    dev_coords = jnp.moveaxis(coords.reshape(DIMS, N_LEAF, PTS_DEV), 1, 0)
    dev_values = jnp.moveaxis(right_sides.reshape(RHS, N_LEAF, PTS_DEV), 1, 0)
    dev_proj = projection.reshape(N_LEAF, PTS_DEV, RANK)
    level_w = jnp.einsum("nrp,npk->nrk", dev_values, dev_proj, precision=lax.Precision.HIGHEST)
    level_c = jnp.take_along_axis(dev_coords, skel_index[:, None, :], axis=2)
    far = jnp.zeros((N_LEAF, RHS, PTS_DEV), jnp.float32)
    devices = jnp.arange(N_LEAF, dtype=jnp.int32)
    for level in range(LEVELS):
        def far_one(inputs):
            device, targets = inputs
            partner = jnp.bitwise_xor(device // (2 ** level), 1)
            far_c = level_c[partner]
            far_w = level_w[partner]
            return jnp.dot(far_w, kernel_block(far_c, targets), precision=lax.Precision.HIGHEST)

        far = far + lax.map(far_one, (devices, dev_coords))
        if level < LEVELS - 1:
            count = N_LEAF // (2 ** (level + 1))
            offset = N_LEAF - N_LEAF // (2 ** level)
            pair_c = level_c.reshape(count, 2, DIMS, RANK)
            pair_w = level_w.reshape(count, 2, RHS, RANK)
            joined_c = jnp.concatenate([pair_c[:, 0], pair_c[:, 1]], axis=2)
            joined_w = jnp.concatenate([pair_w[:, 0], pair_w[:, 1]], axis=2)
            picked = selection[offset:offset + count]
            level_c = jnp.take_along_axis(joined_c, picked[:, None, :], axis=2)
            level_w = jnp.einsum("nrj,jk->nrk", joined_w, transfer, precision=lax.Precision.HIGHEST)
    far = jnp.moveaxis(far, 0, 1).reshape(RHS, POINTS)
    return (near + far) * (1.0 / (NEAR * LEAF) ** 0.5)
```

```python
import functools

import jax
import jax.numpy as jnp
from jax import lax
from jax.experimental import pallas as pl
from jax.experimental.pallas import tpu as pltpu
from jax.sharding import PartitionSpec as P

CENTRE = 2.0
SCALE = 1.4426950408889634**0.5
PAIRS = ((0, 0), (0, 1), (1, 0), (1, 1), (0, 2), (2, 0))
DEPTH = 64
HALF = jnp.bfloat16
GROUP = 4
MESH = pl.DeviceIdType.MESH


def mm(left, right):
    return jnp.dot(left, right, preferred_element_type=jnp.float32)


def scaled_rows(coords):
    x = (coords - CENTRE) * SCALE
    norm = jnp.sum(x * x, axis=0, keepdims=True) * -0.5
    return jnp.concatenate([x, norm, norm], axis=0)


def parts_of(rows):
    parts = []
    for _ in range(3):
        part = rows.astype(HALF).astype(jnp.float32)
        parts.append(part)
        rows = rows - part
    return parts


def columns(rows, source):
    parts = parts_of(rows)
    row = lax.broadcasted_iota(jnp.int32, (8, rows.shape[1]), 0)
    own_row, other_row = (6, 7) if source else (7, 6)
    out = []
    for pair in PAIRS:
        own, other = pair if source else pair[::-1]
        kept = row < 6
        if other == 0:
            kept = kept | (row == own_row)
        block = jnp.where(kept, parts[own], 0.0)
        if own == 0:
            block = jnp.where(row == other_row, 1.0, block)
        out.append(block)
    return out


def halves(value):
    high = value.astype(HALF)
    return high, (value - high.astype(jnp.float32)).astype(HALF)


def stacked(value):
    return jnp.concatenate(halves(value), axis=0)


def folded(total):
    return total[:8] + total[8:]


def source_rows(rows):
    return jnp.concatenate(columns(rows, True) + [rows, jnp.zeros_like(rows)], axis=0).T


RAW = 8 * len(PAIRS)


def kernel(
    coords,
    right,
    projection,
    skel,
    selection,
    transfer,
    near_leaf,
    near_count,
    out,
    got_c,
    got_x,
    proj,
    own_rows,
    picked_rows,
    src_a,
    src_w,
    tgt_b,
    far_a,
    far_w,
    sent,
    got,
    moves,
    exps,
    proj_sem,
    side_send,
    side_recv,
    tree_send,
    tree_recv,
):
    me = lax.axis_index("leaf")
    devices = lax.axis_size("leaf")
    levels = devices.bit_length() - 1
    dims, pts = coords.shape
    leaves, slots = near_leaf.shape
    leaf = pts // leaves
    rank = transfer.shape[1]
    groups = leaves // GROUP
    left, right_of = lax.rem(me + devices - 1, devices), lax.rem(me + 1, devices)

    def partner(level):
        stride = 2**level
        return me + stride * (1 - 2 * ((me // stride) % 2))

    chunks = proj_sem.shape[0]
    rows_of = pts // chunks
    loads = []
    for c in range(chunks):
        at = pl.ds(c * rows_of, rows_of)
        load = pltpu.make_async_copy(projection.at[at, :], proj.at[at, :], proj_sem.at[c])
        load.start()
        loads.append(load)

    barrier = pltpu.get_barrier_semaphore()
    greeted = [left, right_of] + [partner(level) for level in range(levels)]
    for device in greeted:
        pl.semaphore_signal(barrier, inc=1, device_id=(device,), device_id_type=MESH)
    pl.semaphore_wait(barrier, len(greeted))

    sides = []
    for slot, device in ((0, right_of), (1, left)):
        for which, (src, dst) in enumerate(((coords, got_c), (right, got_x))):
            copy = pltpu.make_async_remote_copy(
                src_ref=src,
                dst_ref=dst.at[slot],
                send_sem=side_send.at[slot, which],
                recv_sem=side_recv.at[slot, which],
                device_id=(device,),
                device_id_type=MESH,
            )
            copy.start()
            sides.append(copy)

    def prepare_own(g, carry):
        at = pl.ds(pl.multiple_of(g * leaf, leaf), leaf)
        rows = scaled_rows(coords[:, at])
        turned = source_rows(rows)
        own_rows[at, :] = turned
        src_a[leaves + g] = turned.astype(HALF)
        target = columns(rows, False)
        fill = jnp.zeros((DEPTH - 8 * len(target), leaf), jnp.float32)
        tgt_b[:, at] = jnp.concatenate(target + [fill], axis=0).astype(HALF)
        src_w[leaves + g] = stacked(right[:, at])
        return carry

    lax.fori_loop(0, leaves, prepare_own, 0, unroll=4)

    def pick(i, carry):
        picked_rows[pl.ds(i, 1), :] = own_rows[pl.ds(jnp.clip(skel[0, i], 0, pts - 1), 1), :]
        return carry

    lax.fori_loop(0, rank, pick, 0, unroll=16)
    sent[0, 0:8, :] = picked_rows[...].T[RAW : RAW + 8, :]
    per_chunk = leaves // chunks
    weights = jnp.zeros((16, rank), jnp.float32)
    for c in range(chunks):
        loads[c].wait()

        def project(g, total, c=c):
            at = pl.ds(pl.multiple_of((c * per_chunk + g) * leaf, leaf), leaf)
            high, low = halves(proj[at, :])
            w = src_w[leaves + c * per_chunk + g]
            return total + mm(w, high) + mm(w, low)

        weights = lax.fori_loop(0, per_chunk, project, weights, unroll=True)
    sent[0, 8:16, :] = folded(weights)

    def tree_copy(level):
        return pltpu.make_async_remote_copy(
            src_ref=sent.at[level],
            dst_ref=got.at[level],
            send_sem=tree_send.at[level],
            recv_sem=tree_recv.at[level],
            device_id=(partner(level),),
            device_id_type=MESH,
        )

    tree_copy(0).start()

    moves[0], moves[1] = halves(transfer[...])

    for copy in sides:
        copy.wait_recv()
    for slot in range(2):

        def prepare_side(g, carry, slot=slot):
            at = pl.ds(pl.multiple_of(g * leaf, leaf), leaf)
            src_a[2 * leaves * slot + g] = source_rows(scaled_rows(got_c[slot, :, at])).astype(HALF)
            src_w[2 * leaves * slot + g] = stacked(got_x[slot, :, at])
            return carry

        lax.fori_loop(0, leaves, prepare_side, 0, unroll=4)

    def climb(level):
        tree_copy(level).wait_recv()
        far_c, far_x = got[level, 0:8, :], got[level, 8:16, :]
        far_a[level] = source_rows(far_c).astype(HALF)
        far_w[level] = stacked(far_x)
        if level == levels - 1:
            return
        own_c, own_x = sent[level, 0:8, :], sent[level, 8:16, :]
        upper = (me // 2**level) % 2 == 1
        joined_c = jnp.concatenate([jnp.where(upper, far_c, own_c), jnp.where(upper, own_c, far_c)], axis=1)
        joined_x = jnp.concatenate([jnp.where(upper, far_x, own_x), jnp.where(upper, own_x, far_x)], axis=1)
        row = devices - devices // 2**level + me // 2 ** (level + 1)
        wanted = selection[pl.ds(row, 1), :]
        place = lax.broadcasted_iota(jnp.int32, (2 * rank, rank), 0)
        one_hot = jnp.where(place == wanted, 1.0, 0.0).astype(HALF)
        high, mid = halves(joined_c)
        low = (joined_c - high.astype(jnp.float32) - mid.astype(jnp.float32)).astype(HALF)
        taken = mm(jnp.concatenate([high, mid, low, jnp.zeros_like(low)], axis=0), one_hot)
        sent[level + 1, 0:8, :] = taken[0:8] + taken[8:16] + taken[16:24]
        w = stacked(joined_x)
        sent[level + 1, 8:16, :] = folded(mm(w, moves[0]) + mm(w, moves[1]))
        tree_copy(level + 1).start()

    def sweep(steps, raise_step, weights_of, width):
        totals = [jnp.zeros((16, leaf), jnp.float32) for _ in range(width)]
        for step in range(steps + 1):
            if step < steps:
                for q in range(width):
                    exps[step % 2, :, q * leaf : (q + 1) * leaf] = raise_step(step, q)
            if step:
                for q in range(width):
                    values = jnp.exp2(exps[(step - 1) % 2, :, q * leaf : (q + 1) * leaf])
                    high, low = halves(values)
                    w = weights_of(step - 1, q)
                    totals[q] = totals[q] + mm(w, high) + mm(w, low)
        return totals

    first_leaf = (me - 1) * leaves

    def source(target, slot):
        return jnp.clip(near_leaf[target, slot] - first_leaf, 0, 3 * leaves - 1)

    def near(group):
        base = group * GROUP

        def targets(q):
            return tgt_b[:, pl.ds(pl.multiple_of((base + q) * leaf, leaf), leaf)]

        def raise_step(slot, q):
            return mm(src_a[source(base + q, slot)], targets(q))

        def weights_of(slot, q):
            w = src_w[source(base + q, slot)]
            return jnp.where(slot < near_count[base + q], w, jnp.zeros_like(w))

        totals = sweep(slots, raise_step, weights_of, GROUP)
        for q in range(GROUP):
            out[:, pl.ds(pl.multiple_of((base + q) * leaf, leaf), leaf)] = folded(totals[q])

    def far(group, carry):
        base = group * GROUP

        def raise_step(level, q):
            return mm(far_a[level], tgt_b[:, pl.ds(pl.multiple_of((base + q) * leaf, leaf), leaf)])

        totals = sweep(levels, raise_step, lambda level, q: far_w[level], GROUP)
        for q in range(GROUP):
            at = pl.ds(pl.multiple_of((base + q) * leaf, leaf), leaf)
            out[:, at] = (out[:, at] + folded(totals[q])) * (1.0 / (slots * leaf) ** 0.5)
        return carry

    for group in range(groups):
        near(group)
        if group < levels:
            climb(group)
    lax.fori_loop(0, groups, far, 0)
    for copy in sides:
        copy.wait_send()
    for level in range(levels):
        tree_copy(level).wait_send()


def body(coords, right_sides, projection, skel_index, selection, transfer, near_leaf, near_count):
    devices = lax.axis_size("leaf")
    levels = devices.bit_length() - 1
    dims, pts = coords.shape
    width = right_sides.shape[0]
    leaves, slots = near_leaf.shape
    leaf = pts // leaves
    rank = projection.shape[1]
    chunks = 8
    values = (slots * leaves * leaf + levels * rank) * pts
    vmem, smem = (pl.BlockSpec(memory_space=s) for s in (pltpu.VMEM, pltpu.SMEM))
    return pl.pallas_call(
        kernel,
        out_shape=jax.ShapeDtypeStruct((width, pts), jnp.float32),
        in_specs=[vmem, vmem, pl.BlockSpec(memory_space=pl.ANY), smem, vmem, vmem, smem, smem],
        out_specs=vmem,
        scratch_shapes=[
            pltpu.VMEM((2, dims, pts), jnp.float32),
            pltpu.VMEM((2, width, pts), jnp.float32),
            pltpu.VMEM((pts, rank), jnp.float32),
            pltpu.VMEM((pts, DEPTH), jnp.float32),
            pltpu.VMEM((rank, DEPTH), jnp.float32),
            pltpu.VMEM((3 * leaves, leaf, DEPTH), HALF),
            pltpu.VMEM((3 * leaves, 2 * width, leaf), HALF),
            pltpu.VMEM((DEPTH, pts), HALF),
            pltpu.VMEM((levels, rank, DEPTH), HALF),
            pltpu.VMEM((levels, 2 * width, rank), HALF),
            pltpu.VMEM((levels, 16, rank), jnp.float32),
            pltpu.VMEM((levels, 16, rank), jnp.float32),
            pltpu.VMEM((2, 2 * rank, rank), HALF),
            pltpu.VMEM((2, leaf, GROUP * leaf), jnp.float32),
            pltpu.SemaphoreType.DMA((chunks,)),
            pltpu.SemaphoreType.DMA((2, 2)),
            pltpu.SemaphoreType.DMA((2, 2)),
            pltpu.SemaphoreType.DMA((levels,)),
            pltpu.SemaphoreType.DMA((levels,)),
        ],
        compiler_params=pltpu.CompilerParams(
            collective_id=0, has_side_effects=True, vmem_limit_bytes=56 * 2**20
        ),
        cost_estimate=pl.CostEstimate(
            flops=2 * values * 14, bytes_accessed=4 * pts * rank, transcendentals=values
        ),
    )(coords, right_sides, projection, skel_index, selection, transfer, near_leaf, near_count)


def solution(mesh):
    return jax.shard_map(
        body,
        mesh=mesh,
        in_specs=(
            P(None, "leaf"),
            P(None, "leaf"),
            P("leaf", None),
            P("leaf", None),
            P(),
            P(),
            P("leaf", None),
            P("leaf"),
        ),
        out_specs=P(None, "leaf"),
        check_vma=False,
    )
```

```python
import functools

import jax
import jax.numpy as jnp
from jax import lax
from jax.experimental import pallas as pl
from jax.experimental.pallas import tpu as pltpu
from jax.sharding import PartitionSpec as P

CENTRE = 2.0
SCALE = 1.4426950408889634**0.5
PAIRS = ((0, 0), (0, 1), (1, 0), (1, 1), (0, 2), (2, 0))
DEPTH = 64
HALF = jnp.bfloat16
GROUP = 4
MESH = pl.DeviceIdType.MESH


def mm(left, right):
    return jnp.dot(left, right, preferred_element_type=jnp.float32)


def scaled_rows(coords):
    x = (coords - CENTRE) * SCALE
    norm = jnp.sum(x * x, axis=0, keepdims=True) * -0.5
    return jnp.concatenate([x, norm, norm], axis=0)


def parts_of(rows):
    parts = []
    for _ in range(3):
        part = rows.astype(HALF).astype(jnp.float32)
        parts.append(part)
        rows = rows - part
    return parts


def columns(rows, source):
    parts = parts_of(rows)
    row = lax.broadcasted_iota(jnp.int32, (8, rows.shape[1]), 0)
    own_row, other_row = (6, 7) if source else (7, 6)
    out = []
    for pair in PAIRS:
        own, other = pair if source else pair[::-1]
        kept = row < 6
        if other == 0:
            kept = kept | (row == own_row)
        block = jnp.where(kept, parts[own], 0.0)
        if own == 0:
            block = jnp.where(row == other_row, 1.0, block)
        out.append(block)
    return out


def halves(value):
    high = value.astype(HALF)
    return high, (value - high.astype(jnp.float32)).astype(HALF)


def stacked(value):
    return jnp.concatenate(halves(value), axis=0)


def folded(total):
    return total[:8] + total[8:]


def source_rows(rows):
    return jnp.concatenate(columns(rows, True) + [rows, jnp.zeros_like(rows)], axis=0).T


RAW = 8 * len(PAIRS)


def kernel(
    coords,
    right,
    projection,
    skel,
    selection,
    transfer,
    near_table,
    near_count,
    out,
    got_c,
    got_x,
    proj,
    own_rows,
    picked_rows,
    src_a,
    src_w,
    tgt_b,
    far_a,
    far_w,
    sent,
    got,
    moves,
    exps,
    near_leaf,
    table_sem,
    proj_sem,
    side_send,
    side_recv,
    tree_send,
    tree_recv,
):
    me = lax.axis_index("leaf")
    devices = lax.axis_size("leaf")
    levels = devices.bit_length() - 1
    dims, pts = coords.shape
    slots, leaves = near_table.shape
    leaf = pts // leaves
    rank = transfer.shape[1]
    groups = leaves // GROUP
    left, right_of = lax.rem(me + devices - 1, devices), lax.rem(me + 1, devices)

    def partner(level):
        stride = 2**level
        return me + stride * (1 - 2 * ((me // stride) % 2))

    chunks = proj_sem.shape[0]
    rows_of = pts // chunks
    loads = []
    for c in range(chunks):
        at = pl.ds(c * rows_of, rows_of)
        load = pltpu.make_async_copy(projection.at[at, :], proj.at[at, :], proj_sem.at[c])
        load.start()
        loads.append(load)

    table = pltpu.make_async_copy(near_table, near_leaf, table_sem)
    table.start()

    barrier = pltpu.get_barrier_semaphore()
    greeted = [left, right_of] + [partner(level) for level in range(levels)]
    for device in greeted:
        pl.semaphore_signal(barrier, inc=1, device_id=(device,), device_id_type=MESH)
    pl.semaphore_wait(barrier, len(greeted))

    pieces = side_send.shape[1]
    per_piece = leaves // pieces
    sides = [[] for _ in range(pieces)]
    for piece in range(pieces):
        at = pl.ds(piece * per_piece * leaf, per_piece * leaf)
        for slot, device in ((0, right_of), (1, left)):
            for which, (src, dst) in enumerate(((coords, got_c), (right, got_x))):
                copy = pltpu.make_async_remote_copy(
                    src_ref=src.at[:, at],
                    dst_ref=dst.at[slot, :, at],
                    send_sem=side_send.at[slot, piece, which],
                    recv_sem=side_recv.at[slot, piece, which],
                    device_id=(device,),
                    device_id_type=MESH,
                )
                copy.start()
                sides[piece].append(copy)

    def prepare_own(g, total):
        at = pl.ds(pl.multiple_of(g * leaf, leaf), leaf)
        rows = scaled_rows(coords[:, at])
        turned = source_rows(rows)
        own_rows[at, :] = turned
        src_a[leaves + g] = turned.astype(HALF)
        target = columns(rows, False)
        fill = jnp.zeros((DEPTH - 8 * len(target), leaf), jnp.float32)
        tgt_b[:, at] = jnp.concatenate(target + [fill], axis=0).astype(HALF)
        w = stacked(right[:, at])
        src_w[leaves + g] = w
        high, low = halves(proj[at, :])
        return total + mm(w, high) + mm(w, low)

    per_chunk = leaves // chunks
    weights = jnp.zeros((16, rank), jnp.float32)
    for c in range(chunks):
        loads[c].wait()
        weights = lax.fori_loop(c * per_chunk, (c + 1) * per_chunk, prepare_own, weights, unroll=True)
    sent[0, 8:16, :] = folded(weights)

    def pick(i, carry):
        picked_rows[pl.ds(i, 1), :] = own_rows[pl.ds(jnp.clip(skel[0, i], 0, pts - 1), 1), :]
        return carry

    lax.fori_loop(0, rank, pick, 0, unroll=16)
    sent[0, 0:8, :] = picked_rows[...].T[RAW : RAW + 8, :]

    def tree_copy(level):
        return pltpu.make_async_remote_copy(
            src_ref=sent.at[level],
            dst_ref=got.at[level],
            send_sem=tree_send.at[level],
            recv_sem=tree_recv.at[level],
            device_id=(partner(level),),
            device_id_type=MESH,
        )

    tree_copy(0).start()

    moves[0], moves[1] = halves(transfer[...])

    def climb(level):
        tree_copy(level).wait_recv()
        far_c, far_x = got[level, 0:8, :], got[level, 8:16, :]
        far_a[level] = source_rows(far_c).astype(HALF)
        far_w[level] = stacked(far_x)
        if level == levels - 1:
            return
        own_c, own_x = sent[level, 0:8, :], sent[level, 8:16, :]
        upper = (me // 2**level) % 2 == 1
        joined_c = jnp.concatenate([jnp.where(upper, far_c, own_c), jnp.where(upper, own_c, far_c)], axis=1)
        joined_x = jnp.concatenate([jnp.where(upper, far_x, own_x), jnp.where(upper, own_x, far_x)], axis=1)
        row = devices - devices // 2**level + me // 2 ** (level + 1)
        wanted = selection[pl.ds(row, 1), :]
        place = lax.broadcasted_iota(jnp.int32, (2 * rank, rank), 0)
        one_hot = jnp.where(place == wanted, 1.0, 0.0).astype(HALF)
        high, mid = halves(joined_c)
        low = (joined_c - high.astype(jnp.float32) - mid.astype(jnp.float32)).astype(HALF)
        taken = mm(jnp.concatenate([high, mid, low, jnp.zeros_like(low)], axis=0), one_hot)
        sent[level + 1, 0:8, :] = taken[0:8] + taken[8:16] + taken[16:24]
        w = stacked(joined_x)
        sent[level + 1, 8:16, :] = folded(mm(w, moves[0]) + mm(w, moves[1]))

    def hand_on(level):
        if level < levels - 1:
            tree_copy(level + 1).start()

    def span(at_leaf):
        return pl.ds(pl.multiple_of(at_leaf * leaf, leaf), leaf)

    first_leaf = (me - 1) * leaves

    def source(target, slot):
        return jnp.clip(near_leaf[slot, target] - first_leaf, 0, 3 * leaves - 1)

    def source_of(unit, q):
        kind, group, at = unit
        target = group * GROUP + q
        if kind == "far":
            return lambda: far_a[at], lambda: far_w[at]
        if kind == "own":
            return lambda: src_a[leaves + target], lambda: src_w[leaves + target]

        def weights():
            w = src_w[source(target, at)]
            return jnp.where(at < near_count[target], w, jnp.zeros_like(w))

        return lambda: src_a[source(target, at)], weights

    def take_side(piece, part, parts):
        if part == 0:
            for copy in sides[piece]:
                copy.wait_recv()
        count = per_piece // parts
        for slot in range(2):
            for i in range(count):
                g = piece * per_piece + part * count + i
                at = pl.ds(g * leaf, leaf)
                src_a[2 * leaves * slot + g] = source_rows(scaled_rows(got_c[slot, :, at])).astype(HALF)
                src_w[2 * leaves * slot + g] = stacked(got_x[slot, :, at])

    early = min(2, levels)
    near_units = [("near", group, slot) for group in range(groups) for slot in range(1, slots)]
    units = [("own", group, 0) for group in range(groups)]
    for level in range(early):
        units += [("far", group, level) for group in range(groups)]
    near_start = len(units)
    units += near_units
    for level in range(early, levels):
        units += [("far", group, level) for group in range(groups)]

    last = {unit[1]: step for step, unit in enumerate(units)}
    events = {}

    def add(step, action):
        events.setdefault(step, []).append(action)

    for level in range(min(early + 1, levels)):
        add((level + 1) * groups - 1, functools.partial(climb, level))
        add((level + 1) * groups - 1, functools.partial(hand_on, level))
    later = range(early + 1, levels)
    for i, level in enumerate(later):
        at = near_start + 8 + i * 12
        add(at, functools.partial(climb, level))
        add(at + 3, functools.partial(hand_on, level))
    parts = 2
    first_side = near_start - groups
    for i in range(pieces * parts):
        add(first_side + i * groups // (pieces * parts), functools.partial(take_side, i // parts, i % parts, parts))
    add(near_start - 1, table.wait)

    totals = None
    for step in range(len(units) + 1):
        if step < len(units):
            for q in range(GROUP):
                rows, _ = source_of(units[step], q)
                exps[step % 2, :, q * leaf : (q + 1) * leaf] = mm(rows(), tgt_b[:, span(units[step][1] * GROUP + q)])
        if step:
            kind, group, which = units[step - 1]
            blocks = []
            for q in range(GROUP):
                values = jnp.exp2(exps[(step - 1) % 2, :, q * leaf : (q + 1) * leaf])
                high, low = halves(values)
                w = source_of(units[step - 1], q)[1]()
                blocks.append(mm(w, high) + mm(w, low))
            totals = blocks if totals is None else [t + b for t, b in zip(totals, blocks)]
            if kind != "near" or which == slots - 1:
                for q in range(GROUP):
                    at = span(group * GROUP + q)
                    total = folded(totals[q])
                    if kind != "own":
                        total = out[:, at] + total
                    if last[group] == step - 1:
                        total = total * (1.0 / (slots * leaf) ** 0.5)
                    out[:, at] = total
                totals = None
        for action in events.pop(step, ()):
            action()

    for piece in sides:
        for copy in piece:
            copy.wait_send()
    for level in range(levels):
        tree_copy(level).wait_send()


def body(coords, right_sides, projection, skel_index, selection, transfer, near_leaf, near_count):
    devices = lax.axis_size("leaf")
    levels = devices.bit_length() - 1
    dims, pts = coords.shape
    width = right_sides.shape[0]
    leaves, slots = near_leaf.shape
    leaf = pts // leaves
    rank = projection.shape[1]
    chunks = 8
    pieces = 4
    values = (slots * leaves * leaf + levels * rank) * pts
    vmem, smem = (pl.BlockSpec(memory_space=s) for s in (pltpu.VMEM, pltpu.SMEM))
    return pl.pallas_call(
        kernel,
        out_shape=jax.ShapeDtypeStruct((width, pts), jnp.float32),
        in_specs=[vmem, vmem, pl.BlockSpec(memory_space=pl.ANY), smem, vmem, vmem, vmem, smem],
        out_specs=vmem,
        scratch_shapes=[
            pltpu.VMEM((2, dims, pts), jnp.float32),
            pltpu.VMEM((2, width, pts), jnp.float32),
            pltpu.VMEM((pts, rank), jnp.float32),
            pltpu.VMEM((pts, DEPTH), jnp.float32),
            pltpu.VMEM((rank, DEPTH), jnp.float32),
            pltpu.VMEM((3 * leaves, leaf, DEPTH), HALF),
            pltpu.VMEM((3 * leaves, 2 * width, leaf), HALF),
            pltpu.VMEM((DEPTH, pts), HALF),
            pltpu.VMEM((levels, rank, DEPTH), HALF),
            pltpu.VMEM((levels, 2 * width, rank), HALF),
            pltpu.VMEM((levels, 16, rank), jnp.float32),
            pltpu.VMEM((levels, 16, rank), jnp.float32),
            pltpu.VMEM((2, 2 * rank, rank), HALF),
            pltpu.VMEM((2, leaf, GROUP * leaf), jnp.float32),
            pltpu.SMEM((slots, leaves), jnp.int32),
            pltpu.SemaphoreType.DMA,
            pltpu.SemaphoreType.DMA((chunks,)),
            pltpu.SemaphoreType.DMA((2, pieces, 2)),
            pltpu.SemaphoreType.DMA((2, pieces, 2)),
            pltpu.SemaphoreType.DMA((levels,)),
            pltpu.SemaphoreType.DMA((levels,)),
        ],
        compiler_params=pltpu.CompilerParams(
            collective_id=0, has_side_effects=True, vmem_limit_bytes=56 * 2**20
        ),
        cost_estimate=pl.CostEstimate(
            flops=2 * values * 14, bytes_accessed=4 * pts * rank, transcendentals=values
        ),
    )(coords, right_sides, projection, skel_index, selection, transfer, near_leaf.T, near_count)


def solution(mesh):
    return jax.shard_map(
        body,
        mesh=mesh,
        in_specs=(
            P(None, "leaf"),
            P(None, "leaf"),
            P("leaf", None),
            P("leaf", None),
            P(),
            P(),
            P("leaf", None),
            P("leaf"),
        ),
        out_specs=P(None, "leaf"),
        check_vma=False,
    )
```

```python
import functools

import jax
import jax.numpy as jnp
from jax import lax
from jax.experimental import pallas as pl
from jax.experimental.pallas import tpu as pltpu
from jax.sharding import PartitionSpec as P

CENTRE = 2.0
SCALE = 1.4426950408889634**0.5
PAIRS = ((0, 0), (0, 1), (1, 0), (1, 1), (0, 2), (2, 0))
DEPTH = 64
HALF = jnp.bfloat16
GROUP = 4
MESH = pl.DeviceIdType.MESH


def mm(left, right):
    return jnp.dot(left, right, preferred_element_type=jnp.float32)


def scaled_rows(coords):
    x = (coords - CENTRE) * SCALE
    norm = jnp.sum(x * x, axis=0, keepdims=True) * -0.5
    return jnp.concatenate([x, norm, norm], axis=0)


def parts_of(rows):
    parts = []
    for _ in range(3):
        part = rows.astype(HALF).astype(jnp.float32)
        parts.append(part)
        rows = rows - part
    return parts


def columns(rows, source):
    parts = parts_of(rows)
    row = lax.broadcasted_iota(jnp.int32, (8, rows.shape[1]), 0)
    own_row, other_row = (6, 7) if source else (7, 6)
    out = []
    for pair in PAIRS:
        own, other = pair if source else pair[::-1]
        kept = row < 6
        if other == 0:
            kept = kept | (row == own_row)
        block = jnp.where(kept, parts[own], 0.0)
        if own == 0:
            block = jnp.where(row == other_row, 1.0, block)
        out.append(block)
    return out


def halves(value):
    high = value.astype(HALF)
    return high, (value - high.astype(jnp.float32)).astype(HALF)


def stacked(value):
    return jnp.concatenate(halves(value), axis=0)


def folded(total):
    return total[:8] + total[8:]


def source_rows(rows):
    return jnp.concatenate(columns(rows, True) + [rows, jnp.zeros_like(rows)], axis=0).T


RAW = 8 * len(PAIRS)


def kernel(
    coords,
    right,
    projection,
    skel,
    selection,
    transfer,
    near_table,
    near_count,
    out,
    got_c,
    got_x,
    proj,
    own_rows,
    picked_rows,
    src_a,
    src_w,
    tgt_b,
    far_a,
    far_w,
    sent,
    got,
    moves,
    exps,
    near_leaf,
    table_sem,
    proj_sem,
    side_send,
    side_recv,
    tree_send,
    tree_recv,
):
    me = lax.axis_index("leaf")
    devices = lax.axis_size("leaf")
    levels = devices.bit_length() - 1
    dims, pts = coords.shape
    slots, leaves = near_table.shape
    leaf = pts // leaves
    rank = transfer.shape[1]
    groups = leaves // GROUP
    left, right_of = lax.rem(me + devices - 1, devices), lax.rem(me + 1, devices)

    def partner(level):
        stride = 2**level
        return me + stride * (1 - 2 * ((me // stride) % 2))

    chunks = proj_sem.shape[0]
    rows_of = pts // chunks
    loads = []
    for c in range(chunks):
        at = pl.ds(c * rows_of, rows_of)
        load = pltpu.make_async_copy(projection.at[at, :], proj.at[at, :], proj_sem.at[c])
        load.start()
        loads.append(load)

    table = pltpu.make_async_copy(near_table, near_leaf, table_sem)
    table.start()

    barrier = pltpu.get_barrier_semaphore()
    greeted = [left, right_of] + [partner(level) for level in range(levels)]
    for device in greeted:
        pl.semaphore_signal(barrier, inc=1, device_id=(device,), device_id_type=MESH)
    pl.semaphore_wait(barrier, len(greeted))

    pieces = side_send.shape[1]
    per_piece = leaves // pieces
    sides = [[] for _ in range(pieces)]
    for piece in range(pieces):
        at = pl.ds(piece * per_piece * leaf, per_piece * leaf)
        for slot, device in ((0, right_of), (1, left)):
            for which, (src, dst) in enumerate(((coords, got_c), (right, got_x))):
                copy = pltpu.make_async_remote_copy(
                    src_ref=src.at[:, at],
                    dst_ref=dst.at[slot, :, at],
                    send_sem=side_send.at[slot, piece, which],
                    recv_sem=side_recv.at[slot, piece, which],
                    device_id=(device,),
                    device_id_type=MESH,
                )
                copy.start()
                sides[piece].append(copy)

    def prepare_own(g, total):
        at = pl.ds(pl.multiple_of(g * leaf, leaf), leaf)
        rows = scaled_rows(coords[:, at])
        turned = source_rows(rows)
        own_rows[at, :] = turned
        src_a[leaves + g] = turned.astype(HALF)
        target = columns(rows, False)
        fill = jnp.zeros((DEPTH - 8 * len(target), leaf), jnp.float32)
        tgt_b[:, at] = jnp.concatenate(target + [fill], axis=0).astype(HALF)
        w = stacked(right[:, at])
        src_w[leaves + g] = w
        high, low = halves(proj[at, :])
        return total + mm(w, high) + mm(w, low)

    per_chunk = leaves // chunks
    weights = jnp.zeros((16, rank), jnp.float32)
    for c in range(chunks):
        loads[c].wait()
        weights = lax.fori_loop(c * per_chunk, (c + 1) * per_chunk, prepare_own, weights, unroll=True)
    sent[0, 8:16, :] = folded(weights)

    def pick(i, carry):
        picked_rows[pl.ds(i, 1), :] = own_rows[pl.ds(jnp.clip(skel[0, i], 0, pts - 1), 1), :]
        return carry

    lax.fori_loop(0, rank, pick, 0, unroll=16)
    sent[0, 0:8, :] = picked_rows[...].T[RAW : RAW + 8, :]

    def tree_copy(level):
        return pltpu.make_async_remote_copy(
            src_ref=sent.at[level],
            dst_ref=got.at[level],
            send_sem=tree_send.at[level],
            recv_sem=tree_recv.at[level],
            device_id=(partner(level),),
            device_id_type=MESH,
        )

    tree_copy(0).start()

    moves[0], moves[1] = halves(transfer[...])

    def climb(level):
        tree_copy(level).wait_recv()
        far_c, far_x = got[level, 0:8, :], got[level, 8:16, :]
        far_a[level] = source_rows(far_c).astype(HALF)
        far_w[level] = stacked(far_x)
        if level == levels - 1:
            return
        own_c, own_x = sent[level, 0:8, :], sent[level, 8:16, :]
        upper = (me // 2**level) % 2 == 1
        joined_c = jnp.concatenate([jnp.where(upper, far_c, own_c), jnp.where(upper, own_c, far_c)], axis=1)
        joined_x = jnp.concatenate([jnp.where(upper, far_x, own_x), jnp.where(upper, own_x, far_x)], axis=1)
        row = devices - devices // 2**level + me // 2 ** (level + 1)
        wanted = selection[pl.ds(row, 1), :]
        place = lax.broadcasted_iota(jnp.int32, (2 * rank, rank), 0)
        one_hot = jnp.where(place == wanted, 1.0, 0.0).astype(HALF)
        high, mid = halves(joined_c)
        low = (joined_c - high.astype(jnp.float32) - mid.astype(jnp.float32)).astype(HALF)
        taken = mm(jnp.concatenate([high, mid, low, jnp.zeros_like(low)], axis=0), one_hot)
        sent[level + 1, 0:8, :] = taken[0:8] + taken[8:16] + taken[16:24]
        w = stacked(joined_x)
        sent[level + 1, 8:16, :] = folded(mm(w, moves[0]) + mm(w, moves[1]))

    def hand_on(level):
        if level < levels - 1:
            tree_copy(level + 1).start()

    def span(at_leaf):
        return pl.ds(pl.multiple_of(at_leaf * leaf, leaf), leaf)

    first_leaf = (me - 1) * leaves

    def source(target, slot):
        return jnp.clip(near_leaf[slot, target] - first_leaf, 0, 3 * leaves - 1)

    def source_of(unit, q):
        kind, group, at = unit
        target = group * GROUP + q
        if kind == "far":
            return lambda: far_a[at], lambda: far_w[at]
        if kind == "own":
            return lambda: src_a[leaves + target], lambda: src_w[leaves + target]

        def weights():
            w = src_w[source(target, at)]
            return jnp.where(at < near_count[target], w, jnp.zeros_like(w))

        return lambda: src_a[source(target, at)], weights

    def take_side(piece, part, parts):
        if part == 0:
            for copy in sides[piece]:
                copy.wait_recv()
        count = per_piece // parts
        for slot in range(2):
            for i in range(count):
                g = piece * per_piece + part * count + i
                at = pl.ds(g * leaf, leaf)
                src_a[2 * leaves * slot + g] = source_rows(scaled_rows(got_c[slot, :, at])).astype(HALF)
                src_w[2 * leaves * slot + g] = stacked(got_x[slot, :, at])

    early = min(1, levels)
    near_units = [("near", group, slot) for group in range(groups) for slot in range(1, slots)]
    units = [("own", group, 0) for group in range(groups)]
    for level in range(early):
        units += [("far", group, level) for group in range(groups)]
    near_start = len(units)
    units += near_units
    units += [("far", group, level) for group in range(groups) for level in range(early, levels)]

    last = {unit[1]: step for step, unit in enumerate(units)}
    events = {}

    def add(step, action):
        events.setdefault(step, []).append(action)

    for level in range(min(early + 1, levels)):
        add((level + 1) * groups - 1, functools.partial(climb, level))
        add((level + 1) * groups - 1, functools.partial(hand_on, level))
    later = range(early + 1, levels)
    for i, level in enumerate(later):
        at = near_start + 8 + i * 11
        add(at, functools.partial(climb, level))
        add(at + 3, functools.partial(hand_on, level))
    parts = 2
    first_side = near_start - groups
    for i in range(pieces * parts):
        add(first_side + i * groups // (pieces * parts), functools.partial(take_side, i // parts, i % parts, parts))
    add(near_start - 1, table.wait)

    totals = None
    for step in range(len(units) + 1):
        if step < len(units):
            for q in range(GROUP):
                rows, _ = source_of(units[step], q)
                exps[step % 2, :, q * leaf : (q + 1) * leaf] = mm(rows(), tgt_b[:, span(units[step][1] * GROUP + q)])
        if step:
            kind, group, which = units[step - 1]
            blocks = []
            for q in range(GROUP):
                values = jnp.exp2(exps[(step - 1) % 2, :, q * leaf : (q + 1) * leaf])
                high, low = halves(values)
                w = source_of(units[step - 1], q)[1]()
                blocks.append(mm(w, high) + mm(w, low))
            totals = blocks if totals is None else [t + b for t, b in zip(totals, blocks)]
            if step == len(units) or units[step][:2] != (kind, group):
                for q in range(GROUP):
                    at = span(group * GROUP + q)
                    total = folded(totals[q])
                    if kind != "own":
                        total = out[:, at] + total
                    if last[group] == step - 1:
                        total = total * (1.0 / (slots * leaf) ** 0.5)
                    out[:, at] = total
                totals = None
        for action in events.pop(step, ()):
            action()

    for piece in sides:
        for copy in piece:
            copy.wait_send()
    for level in range(levels):
        tree_copy(level).wait_send()


def body(coords, right_sides, projection, skel_index, selection, transfer, near_leaf, near_count):
    devices = lax.axis_size("leaf")
    levels = devices.bit_length() - 1
    dims, pts = coords.shape
    width = right_sides.shape[0]
    leaves, slots = near_leaf.shape
    leaf = pts // leaves
    rank = projection.shape[1]
    chunks = 8
    pieces = 4
    values = (slots * leaves * leaf + levels * rank) * pts
    vmem, smem = (pl.BlockSpec(memory_space=s) for s in (pltpu.VMEM, pltpu.SMEM))
    return pl.pallas_call(
        kernel,
        out_shape=jax.ShapeDtypeStruct((width, pts), jnp.float32),
        in_specs=[vmem, vmem, pl.BlockSpec(memory_space=pl.ANY), smem, vmem, vmem, vmem, smem],
        out_specs=vmem,
        scratch_shapes=[
            pltpu.VMEM((2, dims, pts), jnp.float32),
            pltpu.VMEM((2, width, pts), jnp.float32),
            pltpu.VMEM((pts, rank), jnp.float32),
            pltpu.VMEM((pts, DEPTH), jnp.float32),
            pltpu.VMEM((rank, DEPTH), jnp.float32),
            pltpu.VMEM((3 * leaves, leaf, DEPTH), HALF),
            pltpu.VMEM((3 * leaves, 2 * width, leaf), HALF),
            pltpu.VMEM((DEPTH, pts), HALF),
            pltpu.VMEM((levels, rank, DEPTH), HALF),
            pltpu.VMEM((levels, 2 * width, rank), HALF),
            pltpu.VMEM((levels, 16, rank), jnp.float32),
            pltpu.VMEM((levels, 16, rank), jnp.float32),
            pltpu.VMEM((2, 2 * rank, rank), HALF),
            pltpu.VMEM((2, leaf, GROUP * leaf), jnp.float32),
            pltpu.SMEM((slots, leaves), jnp.int32),
            pltpu.SemaphoreType.DMA,
            pltpu.SemaphoreType.DMA((chunks,)),
            pltpu.SemaphoreType.DMA((2, pieces, 2)),
            pltpu.SemaphoreType.DMA((2, pieces, 2)),
            pltpu.SemaphoreType.DMA((levels,)),
            pltpu.SemaphoreType.DMA((levels,)),
        ],
        compiler_params=pltpu.CompilerParams(
            collective_id=0, has_side_effects=True, vmem_limit_bytes=56 * 2**20
        ),
        cost_estimate=pl.CostEstimate(
            flops=2 * values * 14, bytes_accessed=4 * pts * rank, transcendentals=values
        ),
    )(coords, right_sides, projection, skel_index, selection, transfer, near_leaf.T, near_count)


def solution(mesh):
    return jax.shard_map(
        body,
        mesh=mesh,
        in_specs=(
            P(None, "leaf"),
            P(None, "leaf"),
            P("leaf", None),
            P("leaf", None),
            P(),
            P(),
            P("leaf", None),
            P("leaf"),
        ),
        out_specs=P(None, "leaf"),
        check_vma=False,
    )
```
